32 devices in a mesh: rep: 4 (over y, x), shard: 8 (over z, core).
Axes of the slice: x: 2, y: 2, z: 4, core: 2. Of those that a mesh axis runs over, the one named last changes fastest.
Arguments:
- inner_wqkv: float32 [4, 2048, 4096], P('rep', 'shard'), may hold values from -8.5 to 8.5
- inner_w1: float32 [4, 2048, 6144], P('rep', 'shard'), may hold values from -8.5 to 8.5
- inner_w3: float32 [4, 2048, 6144], P('rep', 'shard'), may hold values from -8.5 to 8.5
- inner_wo: float32 [4, 2048, 2048], P('rep', 'shard'), may hold values from -8.5 to 8.5
- inner_w2: float32 [4, 6144, 2048], P('rep', 'shard'), may hold values from -8.5 to 8.5
- outer_wqkv: float32 [2048, 4096], P('shard', 'rep'), may hold values from -8 to 8
- outer_w1: float32 [2048, 6144], P('shard', 'rep'), may hold values from -8 to 8
- outer_w3: float32 [2048, 6144], P('shard', 'rep'), may hold values from -8 to 8
- outer_wo: float32 [2048, 2048], P('shard', 'rep'), may hold values from -8 to 8
- outer_w2: float32 [6144, 2048], P('shard', 'rep'), may hold values from -8 to 8
- moment_wqkv: float32 [2048, 4096], P('shard', 'rep'), may hold values from -0.4 to 0.4
- moment_w1: float32 [2048, 6144], P('shard', 'rep'), may hold values from -0.4 to 0.4
- moment_w3: float32 [2048, 6144], P('shard', 'rep'), may hold values from -0.4 to 0.4
- moment_wo: float32 [2048, 2048], P('shard', 'rep'), may hold values from -0.4 to 0.4
- moment_w2: float32 [6144, 2048], P('shard', 'rep'), may hold values from -0.4 to 0.4
- basis_wo: float32 [2048, 64], P('shard'), may hold values from -0.5 to 0.5
- basis_w2: float32 [6144, 64], P('shard'), may hold values from -0.3125 to 0.3125
Outputs:
- weights_wqkv: bfloat16 [2048, 4096], P('shard')
- weights_w1: bfloat16 [2048, 6144], P('shard')
- weights_w3: bfloat16 [2048, 6144], P('shard')
- weights_wo: bfloat16 [2048, 2048], P('shard')
- weights_w2: bfloat16 [6144, 2048], P('shard')
- master_wqkv: float32 [2048, 4096], P('shard', 'rep')
- master_w1: float32 [2048, 6144], P('shard', 'rep')
- master_w3: float32 [2048, 6144], P('shard', 'rep')
- master_wo: float32 [2048, 2048], P('shard', 'rep')
- master_w2: float32 [6144, 2048], P('shard', 'rep')
- momentum_wqkv: float32 [2048, 4096], P('shard', 'rep')
- momentum_w1: float32 [2048, 6144], P('shard', 'rep')
- momentum_w3: float32 [2048, 6144], P('shard', 'rep')
- momentum_wo: float32 [2048, 2048], P('shard', 'rep')
- momentum_w2: float32 [6144, 2048], P('shard', 'rep')
The draws below stay inside these ranges and needn't reach their ends.
All inputs are finite; a program needn't handle non-finite values.
Results may differ from the reference program's by a relative error of at most 0.007.
Values may be sent and summed in bfloat16 or wider, within the bound.
A program may use at most 128 MiB of HBM per device.

```python
import jax
import jax.numpy as jnp
from jax import lax

D = 2048
FF = 6144
RANK = 64
QKV = 4096
GROUPS = 4
N_REP = 4


def outer_field(key, salt, row_count, col_count):
    sub = jax.random.fold_in(key, salt)
    values = jnp.clip(3.0 * jax.random.normal(sub, (row_count, col_count), jnp.float32), -8.0, 8.0)
    return values


def inner_field(key, salt, row_count, col_count):
    base = outer_field(key, salt, row_count, col_count)
    sub = jax.random.fold_in(key, salt + 100)
    noise = jnp.clip(0.1 * jax.random.normal(sub, (GROUPS, row_count, col_count), jnp.float32), -0.5, 0.5)
    return base[None, :, :] + noise


def draw_outer_wqkv(key, part):
    return outer_field(key, 1, D, QKV)


def draw_outer_w1(key, part):
    return outer_field(key, 2, D, FF)


def draw_outer_w3(key, part):
    return outer_field(key, 3, D, FF)


def draw_outer_wo(key, part):
    return outer_field(key, 4, D, D)


def draw_outer_w2(key, part):
    return outer_field(key, 5, FF, D)


def draw_inner_wqkv(key, part):
    return inner_field(key, 1, D, QKV)


def draw_inner_w1(key, part):
    return inner_field(key, 2, D, FF)


def draw_inner_w3(key, part):
    return inner_field(key, 3, D, FF)


def draw_inner_wo(key, part):
    return inner_field(key, 4, D, D)


def draw_inner_w2(key, part):
    return inner_field(key, 5, FF, D)


def levels(rng, shape, split, low, high):
    loudness = 1.0
    for axis_at, blocks in split:
        draws = jax.random.uniform(jax.random.fold_in(jax.random.fold_in(rng, 6), axis_at), (blocks,), jnp.float32, low / len(split), high / len(split))
        loudness = loudness * jnp.repeat(jnp.exp(draws), shape[axis_at] // blocks).reshape((-1,) + (1,) * (len(shape) - 1 - axis_at))
    return loudness


def centred(key, shape, scale, limit, shards=(), dtype=jnp.bfloat16):
    result = scale * jax.random.normal(key, shape, jnp.float32)
    if shards:
        result = result * levels(key, shape, shards, -0.22, 0.18)
    return jnp.clip(result, -limit, limit).astype(dtype)


def setup_inputs(seed: int = 0) -> dict:
    splits = jax.random.split(jax.random.key(seed), 18)
    return {
        "inner_wqkv": draw_inner_wqkv(jax.random.fold_in(splits[17], 71), 0),
        "inner_w1": draw_inner_w1(jax.random.fold_in(splits[17], 71), 0),
        "inner_w3": draw_inner_w3(jax.random.fold_in(splits[17], 71), 0),
        "inner_wo": draw_inner_wo(jax.random.fold_in(splits[17], 71), 0),
        "inner_w2": draw_inner_w2(jax.random.fold_in(splits[17], 71), 0),
        "outer_wqkv": draw_outer_wqkv(jax.random.fold_in(splits[17], 71), 0),
        "outer_w1": draw_outer_w1(jax.random.fold_in(splits[17], 71), 0),
        "outer_w3": draw_outer_w3(jax.random.fold_in(splits[17], 71), 0),
        "outer_wo": draw_outer_wo(jax.random.fold_in(splits[17], 71), 0),
        "outer_w2": draw_outer_w2(jax.random.fold_in(splits[17], 71), 0),
        "moment_wqkv": centred(splits[10], (D, QKV), 0.1, 0.4, ((0, 8), (1, 4)), jnp.float32),
        "moment_w1": centred(splits[11], (D, FF), 0.1, 0.4, ((0, 8), (1, 4)), jnp.float32),
        "moment_w3": centred(splits[12], (D, FF), 0.1, 0.4, ((0, 8), (1, 4)), jnp.float32),
        "moment_wo": centred(splits[13], (D, D), 0.1, 0.4, ((0, 8), (1, 4)), jnp.float32),
        "moment_w2": centred(splits[14], (FF, D), 0.1, 0.4, ((0, 8), (1, 4)), jnp.float32),
        "basis_wo": centred(splits[15], (D, RANK), (D // 16) ** -0.5, 0.5, ((0, 8),), jnp.float32),
        "basis_w2": centred(splits[16], (FF, RANK), (FF // 16) ** -0.5, 0.3125, ((0, 8),), jnp.float32),
    }


rate_outer = 0.7
decay_moment = 0.9


def nesterov(outer, moment, delta):
    moment_new = decay_moment * moment + delta
    master = outer - rate_outer * (delta + decay_moment * moment_new)
    return master.astype(jnp.bfloat16), master, moment_new


def lowrank(inner, outer, basis):
    highest = lax.Precision.HIGHEST
    diff = outer - jnp.sum(inner, axis=0) / N_REP
    coeff = jnp.dot(basis.T, diff, precision=highest, preferred_element_type=jnp.float32)
    return jnp.dot(basis, coeff, precision=highest, preferred_element_type=jnp.float32)


def reference(inner_wqkv, inner_w1, inner_w3, inner_wo, inner_w2, outer_wqkv, outer_w1, outer_w3, outer_wo, outer_w2, moment_wqkv, moment_w1, moment_w3, moment_wo, moment_w2, basis_wo, basis_w2):
    d_qkv = outer_wqkv - jnp.sum(inner_wqkv, axis=0) / N_REP
    d_one = outer_w1 - jnp.sum(inner_w1, axis=0) / N_REP
    d_three = outer_w3 - jnp.sum(inner_w3, axis=0) / N_REP
    d_out = lowrank(inner_wo, outer_wo, basis_wo)
    d_down = lowrank(inner_w2, outer_w2, basis_w2)
    a0, b0, c0 = nesterov(outer_wqkv, moment_wqkv, d_qkv)
    a1, b1, c1 = nesterov(outer_w1, moment_w1, d_one)
    a3, b3, c3 = nesterov(outer_w3, moment_w3, d_three)
    ao, bo, co = nesterov(outer_wo, moment_wo, d_out)
    a2, b2, c2 = nesterov(outer_w2, moment_w2, d_down)
    return (a0, a1, a3, ao, a2, b0, b1, b3, bo, b2, c0, c1, c3, co, c2)
```

```python
import math

import jax
import jax.numpy as jnp
from jax import lax
from jax.experimental import pallas as pl
from jax.experimental.pallas import tpu as pltpu
from jax.sharding import PartitionSpec as P

rate_outer = 0.7
decay_moment = 0.9
inner_limit = 8.5
octaves = 124.0


def project(basis, matrix):
    return lax.dot_general(
        basis,
        matrix,
        (((0,), (0,)), ((), ())),
        precision=lax.Precision.HIGHEST,
        preferred_element_type=jnp.float32,
    )


def rebuild(basis, coeff):
    return jnp.dot(
        basis, coeff, precision=lax.Precision.HIGHEST, preferred_element_type=jnp.float32
    )


def nesterov(outer, moment, delta):
    moment_new = decay_moment * moment + delta
    master = outer - rate_outer * (delta + decay_moment * moment_new)
    return (master.astype(jnp.bfloat16), master, moment_new)


def pack(value, limit):
    slope = 2.0 * octaves * math.log(2.0) / limit
    size = jnp.exp(jnp.abs(value) * slope - octaves * math.log(2.0))
    return jnp.where(value < 0, -size, size).astype(jnp.bfloat16)


def unpack(code, limit):
    slope = limit / (2.0 * octaves * math.log(2.0))
    wide = code.astype(jnp.float32)
    size = (jnp.log(jnp.abs(wide)) + octaves * math.log(2.0)) * slope
    return jnp.where(wide < 0, -size, size)


def keep_wide(value, limit):
    return value


def swap(value, bit, axis):
    return lax.ppermute(value, axis, [(i, i ^ bit) for i in range(lax.axis_size(axis))])


def scatter_pairs(matrix, low, rows, first, second, encode, decode):
    me = lax.axis_index("rep")
    width = matrix.shape[1] // 4

    def block(owner):
        return lax.dynamic_slice(matrix, (low, owner * width), (rows, width))

    far = swap(encode(block(me ^ 3), inner_limit), first, "rep")
    near = swap(encode(block(me ^ first), inner_limit), first, "rep")
    relay = block(me ^ second) + decode(far, inner_limit)
    across = swap(encode(relay, 2 * inner_limit), second, "rep")
    return block(me) + decode(near, inner_limit) + decode(across, 2 * inner_limit)


def sum_columns(matrix):
    if lax.axis_size("rep") != 4:
        return lax.psum_scatter(matrix, "rep", scatter_dimension=1, tiled=True)
    half = matrix.shape[0] // 2
    return jnp.concatenate(
        [
            scatter_pairs(matrix, 0, half, 1, 2, pack, unpack),
            scatter_pairs(matrix, half, half, 2, 1, pack, unpack),
        ],
        axis=0,
    )


def place_kernel(own, by_x, by_y, far_top, far_low, out, sems):
    me = lax.axis_index("rep")
    rows, width = own.shape
    half = rows // 2

    def columns(owner):
        return pl.ds(pl.multiple_of(owner * width, 128), width)

    copies = [
        pltpu.make_async_copy(own, out.at[:, columns(me)], sems.at[0]),
        pltpu.make_async_copy(by_x, out.at[:, columns(me ^ 1)], sems.at[1]),
        pltpu.make_async_copy(by_y, out.at[:, columns(me ^ 2)], sems.at[2]),
        pltpu.make_async_copy(far_top, out.at[pl.ds(0, half), columns(me ^ 3)], sems.at[3]),
        pltpu.make_async_copy(far_low, out.at[pl.ds(half, half), columns(me ^ 3)], sems.at[4]),
    ]
    for copy in copies:
        copy.start()
    for copy in copies:
        copy.wait()


def gather_columns(own):
    if lax.axis_size("rep") != 4:
        return lax.all_gather(own, "rep", axis=1, tiled=True)
    rows, width = own.shape
    half = rows // 2
    by_x = swap(own, 1, "rep")
    by_y = swap(own, 2, "rep")
    far_top = swap(by_x[:half], 2, "rep")
    far_low = swap(by_y[half:], 1, "rep")
    return pl.pallas_call(
        place_kernel,
        out_shape=jax.ShapeDtypeStruct((rows, 4 * width), own.dtype),
        in_specs=[pl.BlockSpec(memory_space=pl.ANY)] * 5,
        out_specs=pl.BlockSpec(memory_space=pl.ANY),
        scratch_shapes=[pltpu.SemaphoreType.DMA((5,))],
        cost_estimate=pl.CostEstimate(
            flops=0, bytes_accessed=16 * rows * width, transcendentals=0
        ),
    )(own, by_x, by_y, far_top, far_low)


def coefficients(inner_out, inner_down, outer_out, outer_down, basis_out, basis_down):
    groups = lax.axis_size("rep")
    parts = (project(basis_out, inner_out), project(basis_down, inner_down))
    if groups == 4:
        rank = parts[0].shape[0]
        out_sum = scatter_pairs(parts[0], 0, rank, 1, 2, keep_wide, keep_wide)
        down_sum = scatter_pairs(parts[1], 0, rank, 2, 1, keep_wide, keep_wide)
    else:
        out_sum, down_sum = [
            lax.psum_scatter(part, "rep", scatter_dimension=1, tiled=True) for part in parts
        ]
    out_term = project(basis_out, outer_out) - out_sum / groups
    down_term = project(basis_down, outer_down) - down_sum / groups
    shards = lax.axis_size("shard")
    if shards & (shards - 1) or shards < 2:
        return lax.psum((out_term, down_term), "shard")
    even = lax.axis_index("shard") % 2 == 0
    total = jnp.where(even, out_term, down_term)
    total = total + swap(jnp.where(even, down_term, out_term), 1, "shard")
    bit = 2
    while bit < shards:
        total = total + swap(total, bit, "shard")
        bit *= 2
    other = swap(total, 1, "shard")
    return jnp.where(even, total, other), jnp.where(even, other, total)


def on_device(
    inner_wqkv,
    inner_w1,
    inner_w3,
    inner_wo,
    inner_w2,
    outer_wqkv,
    outer_w1,
    outer_w3,
    outer_wo,
    outer_w2,
    moment_wqkv,
    moment_w1,
    moment_w3,
    moment_wo,
    moment_w2,
    basis_wo,
    basis_w2,
):
    groups = lax.axis_size("rep")
    d_qkv = outer_wqkv - sum_columns(inner_wqkv[0]) / groups
    coeff_out, coeff_down = coefficients(
        inner_wo[0], inner_w2[0], outer_wo, outer_w2, basis_wo, basis_w2
    )
    d_one = outer_w1 - sum_columns(inner_w1[0]) / groups
    d_three = outer_w3 - sum_columns(inner_w3[0]) / groups
    d_out = rebuild(basis_wo, coeff_out)
    d_down = rebuild(basis_w2, coeff_down)
    a0, b0, c0 = nesterov(outer_wqkv, moment_wqkv, d_qkv)
    a1, b1, c1 = nesterov(outer_w1, moment_w1, d_one)
    a3, b3, c3 = nesterov(outer_w3, moment_w3, d_three)
    ao, bo, co = nesterov(outer_wo, moment_wo, d_out)
    a2, b2, c2 = nesterov(outer_w2, moment_w2, d_down)
    return (
        gather_columns(a0),
        gather_columns(a1),
        gather_columns(a3),
        gather_columns(ao),
        gather_columns(a2),
        b0,
        b1,
        b3,
        bo,
        b2,
        c0,
        c1,
        c3,
        co,
        c2,
    )


def solution(mesh):
    inner = P("rep", "shard", None)
    owned = P("shard", "rep")
    shared = P("shard", None)
    return jax.shard_map(
        on_device,
        mesh=mesh,
        in_specs=(inner,) * 5 + (owned,) * 10 + (shared,) * 2,
        out_specs=(shared,) * 5 + (owned,) * 10,
        check_vma=False,
    )
```

```python
import math

import jax
import jax.numpy as jnp
from jax import lax
from jax.experimental import pallas as pl
from jax.experimental.pallas import tpu as pltpu
from jax.sharding import PartitionSpec as P

rate_outer = 0.7
decay_moment = 0.9
inner_limit = 8.5
octaves = 124.0


def project(basis, matrix):
    return lax.dot_general(
        basis,
        matrix,
        (((0,), (0,)), ((), ())),
        precision=lax.Precision.HIGHEST,
        preferred_element_type=jnp.float32,
    )


def rebuild(basis, coeff):
    return jnp.dot(
        basis, coeff, precision=lax.Precision.HIGHEST, preferred_element_type=jnp.float32
    )


def nesterov(outer, moment, delta):
    moment_new = decay_moment * moment + delta
    master = outer - rate_outer * (delta + decay_moment * moment_new)
    return (master.astype(jnp.bfloat16), master, moment_new)


def pack(value, limit):
    slope = 2.0 * octaves * math.log(2.0) / limit
    size = jnp.exp(jnp.abs(value) * slope - octaves * math.log(2.0))
    return jnp.where(value < 0, -size, size).astype(jnp.bfloat16)


def unpack(code, limit):
    slope = limit / (2.0 * octaves * math.log(2.0))
    wide = code.astype(jnp.float32)
    size = (jnp.log(jnp.abs(wide)) + octaves * math.log(2.0)) * slope
    return jnp.where(wide < 0, -size, size)


def keep_wide(value, limit):
    return value


def swap(value, bit, axis):
    return lax.ppermute(value, axis, [(i, i ^ bit) for i in range(lax.axis_size(axis))])


def scatter_pairs(matrix, low, rows, first, second, encode, decode):
    me = lax.axis_index("rep")
    width = matrix.shape[1] // 4

    def block(owner):
        return lax.dynamic_slice(matrix, (low, owner * width), (rows, width))

    sent = encode(jnp.concatenate([block(me ^ 3), block(me ^ first)], axis=0), inner_limit)
    came = swap(sent, first, "rep")
    far, near = came[:rows], came[rows:]
    relay = block(me ^ second) + decode(far, inner_limit)
    across = swap(encode(relay, 2 * inner_limit), second, "rep")
    return block(me) + decode(near, inner_limit) + decode(across, 2 * inner_limit)


def sum_columns(matrix):
    if lax.axis_size("rep") != 4:
        return lax.psum_scatter(matrix, "rep", scatter_dimension=1, tiled=True)
    half = matrix.shape[0] // 2
    return jnp.concatenate(
        [
            scatter_pairs(matrix, 0, half, 1, 2, pack, unpack),
            scatter_pairs(matrix, half, half, 2, 1, pack, unpack),
        ],
        axis=0,
    )


def place(pieces, low, rows):
    own = pieces[0]
    width = own.shape[1]
    half = own.shape[0] // 2
    tile = math.gcd(math.gcd(half, 128), math.gcd(low, rows))
    start, middle = low // tile, half // tile

    def body(own, by_x, by_y, far_top, far_low, out):
        me = lax.axis_index("rep")

        def columns(owner):
            return pl.ds(pl.multiple_of(owner * width, 128), width)

        out[:, columns(me)] = own[...]
        out[:, columns(me ^ 1)] = by_x[...]
        out[:, columns(me ^ 2)] = by_y[...]
        is_top = pl.program_id(0) + start < middle

        @pl.when(is_top)
        def _():
            out[:, columns(me ^ 3)] = far_top[...]

        @pl.when(jnp.logical_not(is_top))
        def _():
            out[:, columns(me ^ 3)] = far_low[...]

    def whole(i):
        return (i + start, 0)

    def upper(i):
        return (jnp.minimum(i + start, middle - 1), 0)

    def lower(i):
        return (jnp.maximum(i + start - middle, 0), 0)

    return pl.pallas_call(
        body,
        grid=(rows // tile,),
        out_shape=jax.ShapeDtypeStruct((rows, 4 * width), own.dtype),
        in_specs=[pl.BlockSpec((tile, width), m) for m in (whole, whole, whole, upper, lower)],
        out_specs=pl.BlockSpec((tile, 4 * width), lambda i: (i, 0)),
        compiler_params=pltpu.CompilerParams(vmem_limit_bytes=16 * 2**20),
        cost_estimate=pl.CostEstimate(
            flops=0, bytes_accessed=16 * rows * width, transcendentals=0
        ),
    )(*pieces)


def exchange(own):
    half = own.shape[0] // 2
    by_x = swap(own, 1, "rep")
    by_y = swap(own, 2, "rep")
    return own, by_x, by_y, swap(by_x[:half], 2, "rep"), swap(by_y[half:], 1, "rep")


def gather_columns(*parts):
    if lax.axis_size("rep") != 4:
        return [lax.all_gather(part, "rep", axis=1, tiled=True) for part in parts]
    pieces = exchange(jnp.concatenate(parts, axis=0) if len(parts) > 1 else parts[0])
    fresh, low = [], 0
    for part in parts:
        fresh.append(place(pieces, low, part.shape[0]))
        low += part.shape[0]
    return fresh


def coefficients(inner_out, inner_down, outer_out, outer_down, basis_out, basis_down):
    groups = lax.axis_size("rep")
    parts = (project(basis_out, inner_out), project(basis_down, inner_down))
    if groups == 4:
        rank = parts[0].shape[0]
        out_sum = scatter_pairs(parts[0], 0, rank, 1, 2, keep_wide, keep_wide)
        down_sum = scatter_pairs(parts[1], 0, rank, 2, 1, keep_wide, keep_wide)
    else:
        out_sum, down_sum = [
            lax.psum_scatter(part, "rep", scatter_dimension=1, tiled=True) for part in parts
        ]
    out_term = project(basis_out, outer_out) - out_sum / groups
    down_term = project(basis_down, outer_down) - down_sum / groups
    shards = lax.axis_size("shard")
    if shards & (shards - 1) or shards < 2:
        return lax.psum((out_term, down_term), "shard")
    even = lax.axis_index("shard") % 2 == 0
    total = jnp.where(even, out_term, down_term)
    total = total + swap(jnp.where(even, down_term, out_term), 1, "shard")
    bit = 2
    while bit < shards:
        total = total + swap(total, bit, "shard")
        bit *= 2
    other = swap(total, 1, "shard")
    return jnp.where(even, total, other), jnp.where(even, other, total)


def on_device(
    inner_wqkv,
    inner_w1,
    inner_w3,
    inner_wo,
    inner_w2,
    outer_wqkv,
    outer_w1,
    outer_w3,
    outer_wo,
    outer_w2,
    moment_wqkv,
    moment_w1,
    moment_w3,
    moment_wo,
    moment_w2,
    basis_wo,
    basis_w2,
):
    groups = lax.axis_size("rep")
    d_qkv = outer_wqkv - sum_columns(inner_wqkv[0]) / groups
    coeff_out, coeff_down = coefficients(
        inner_wo[0], inner_w2[0], outer_wo, outer_w2, basis_wo, basis_w2
    )
    d_one = outer_w1 - sum_columns(inner_w1[0]) / groups
    d_three = outer_w3 - sum_columns(inner_w3[0]) / groups
    d_out = rebuild(basis_wo, coeff_out)
    d_down = rebuild(basis_w2, coeff_down)
    a0, b0, c0 = nesterov(outer_wqkv, moment_wqkv, d_qkv)
    a1, b1, c1 = nesterov(outer_w1, moment_w1, d_one)
    a3, b3, c3 = nesterov(outer_w3, moment_w3, d_three)
    ao, bo, co = nesterov(outer_wo, moment_wo, d_out)
    a2, b2, c2 = nesterov(outer_w2, moment_w2, d_down)
    (w0,) = gather_columns(a0)
    wo, w2 = gather_columns(ao, a2)
    (w1,) = gather_columns(a1)
    (w3,) = gather_columns(a3)
    return (
        w0,
        w1,
        w3,
        wo,
        w2,
        b0,
        b1,
        b3,
        bo,
        b2,
        c0,
        c1,
        c3,
        co,
        c2,
    )


def solution(mesh):
    inner = P("rep", "shard", None)
    owned = P("shard", "rep")
    shared = P("shard", None)
    return jax.shard_map(
        on_device,
        mesh=mesh,
        in_specs=(inner,) * 5 + (owned,) * 10 + (shared,) * 2,
        out_specs=(shared,) * 5 + (owned,) * 10,
        check_vma=False,
    )
```

```python
import functools
import math

import jax
import jax.numpy as jnp
from jax import lax
from jax.experimental import pallas as pl
from jax.experimental.pallas import tpu as pltpu
from jax.sharding import PartitionSpec as P

rate_outer = 0.7
decay_moment = 0.9
inner_limit = 8.5
octaves = 124.0


def project(basis, matrix):
    return lax.dot_general(
        basis,
        matrix,
        (((0,), (0,)), ((), ())),
        precision=lax.Precision.HIGHEST,
        preferred_element_type=jnp.float32,
    )


def rebuild(basis, coeff):
    return jnp.dot(
        basis, coeff, precision=lax.Precision.HIGHEST, preferred_element_type=jnp.float32
    )


def nesterov(outer, moment, delta):
    moment_new = decay_moment * moment + delta
    master = outer - rate_outer * (delta + decay_moment * moment_new)
    return (master.astype(jnp.bfloat16), master, moment_new)


def pack(value, limit):
    slope = 2.0 * octaves * math.log(2.0) / limit
    size = jnp.exp(jnp.abs(value) * slope - octaves * math.log(2.0))
    return jnp.where(value < 0, -size, size).astype(jnp.bfloat16)


def unpack(code, limit):
    slope = limit / (2.0 * octaves * math.log(2.0))
    wide = code.astype(jnp.float32)
    size = (jnp.log(jnp.abs(wide)) + octaves * math.log(2.0)) * slope
    return jnp.where(wide < 0, -size, size)


def keep_wide(value, limit):
    return value


def swap(value, bit, axis):
    return lax.ppermute(value, axis, [(i, i ^ bit) for i in range(lax.axis_size(axis))])


def scatter_pairs(matrix, low, rows, first, second, encode, decode):
    me = lax.axis_index("rep")
    width = matrix.shape[1] // 4

    def block(owner):
        return lax.dynamic_slice(matrix, (low, owner * width), (rows, width))

    sent = encode(jnp.concatenate([block(me ^ 3), block(me ^ first)], axis=0), inner_limit)
    came = swap(sent, first, "rep")
    far, near = came[:rows], came[rows:]
    relay = block(me ^ second) + decode(far, inner_limit)
    across = swap(encode(relay, 2 * inner_limit), second, "rep")
    return block(me) + decode(near, inner_limit) + decode(across, 2 * inner_limit)


def sum_columns(matrix):
    if lax.axis_size("rep") != 4:
        return lax.psum_scatter(matrix, "rep", scatter_dimension=1, tiled=True)
    half = matrix.shape[0] // 2
    return jnp.concatenate(
        [
            scatter_pairs(matrix, 0, half, 1, 2, pack, unpack),
            scatter_pairs(matrix, half, half, 2, 1, pack, unpack),
        ],
        axis=0,
    )


def place(pieces, low, rows):
    own = pieces[0]
    width = own.shape[1]
    half = own.shape[0] // 2
    tile = math.gcd(math.gcd(half, 128), math.gcd(low, rows))
    start, middle = low // tile, half // tile

    def body(own, by_x, by_y, far_top, far_low, out):
        me = lax.axis_index("rep")

        def columns(owner):
            return pl.ds(pl.multiple_of(owner * width, 128), width)

        out[:, columns(me)] = own[...]
        out[:, columns(me ^ 1)] = by_x[...]
        out[:, columns(me ^ 2)] = by_y[...]
        is_top = pl.program_id(0) + start < middle

        @pl.when(is_top)
        def _():
            out[:, columns(me ^ 3)] = far_top[...]

        @pl.when(jnp.logical_not(is_top))
        def _():
            out[:, columns(me ^ 3)] = far_low[...]

    def whole(i):
        return (i + start, 0)

    def upper(i):
        return (jnp.minimum(i + start, middle - 1), 0)

    def lower(i):
        return (jnp.maximum(i + start - middle, 0), 0)

    return pl.pallas_call(
        body,
        grid=(rows // tile,),
        out_shape=jax.ShapeDtypeStruct((rows, 4 * width), own.dtype),
        in_specs=[pl.BlockSpec((tile, width), m) for m in (whole, whole, whole, upper, lower)],
        out_specs=pl.BlockSpec((tile, 4 * width), lambda i: (i, 0)),
        compiler_params=pltpu.CompilerParams(vmem_limit_bytes=16 * 2**20),
        cost_estimate=pl.CostEstimate(
            flops=0, bytes_accessed=16 * rows * width, transcendentals=0
        ),
    )(*pieces)


def exchange(own):
    half = own.shape[0] // 2
    by_x = swap(own, 1, "rep")
    by_y = swap(own, 2, "rep")
    return own, by_x, by_y, swap(by_x[:half], 2, "rep"), swap(by_y[half:], 1, "rep")


def gather_columns(*parts):
    if lax.axis_size("rep") != 4:
        return [lax.all_gather(part, "rep", axis=1, tiled=True) for part in parts]
    pieces = exchange(jnp.concatenate(parts, axis=0) if len(parts) > 1 else parts[0])
    fresh, low = [], 0
    for part in parts:
        fresh.append(place(pieces, low, part.shape[0]))
        low += part.shape[0]
    return fresh


def coefficients(inner_out, inner_down, outer_out, outer_down, basis_out, basis_down):
    groups = lax.axis_size("rep")
    parts = (project(basis_out, inner_out), project(basis_down, inner_down))
    if groups == 4:
        rank = parts[0].shape[0]
        out_sum = scatter_pairs(parts[0], 0, rank, 1, 2, keep_wide, keep_wide)
        down_sum = scatter_pairs(parts[1], 0, rank, 2, 1, keep_wide, keep_wide)
    else:
        out_sum, down_sum = [
            lax.psum_scatter(part, "rep", scatter_dimension=1, tiled=True) for part in parts
        ]
    out_term = project(basis_out, outer_out) - out_sum / groups
    down_term = project(basis_down, outer_down) - down_sum / groups
    shards = lax.axis_size("shard")
    if shards & (shards - 1) or shards < 2:
        return lax.psum((out_term, down_term), "shard")
    even = lax.axis_index("shard") % 2 == 0
    total = jnp.where(even, out_term, down_term)
    total = total + swap(jnp.where(even, down_term, out_term), 1, "shard")
    bit = 2
    while bit < shards:
        total = total + swap(total, bit, "shard")
        bit *= 2
    other = swap(total, 1, "shard")
    return jnp.where(even, total, other), jnp.where(even, other, total)


def fused_kernel(groups, shards, *refs):
    refs = list(refs)

    def take(n):
        got, refs[:n] = refs[:n], []
        return got

    inner, outer, moment = take(3), take(5), take(5)
    parts, terms, basis = take(2), take(2), take(2)
    weights, master, momentum = take(5), take(5), take(5)
    inner_v, outer_v, moment_v = take(3), take(5), take(5)
    send1, recv1, recv2 = take(3), take(3), take(3)
    own, by_x, by_y, far = take(5), take(5), take(5), take(5)
    c_recv1, c_relay, c_recv2, s_send, s_recv = take(5)
    load_sem, store_sem = take(2)
    rs1, rs2, c1, c2, sh, agx, agy, agf = [take(2) for _ in range(8)]

    rep, shard = lax.axis_index("rep"), lax.axis_index("shard")

    def remote(src, dst, sems, at, rep_bit, shard_bit=0):
        return pltpu.make_async_remote_copy(
            src_ref=src,
            dst_ref=dst,
            send_sem=sems[0].at[at],
            recv_sem=sems[1].at[at],
            device_id=(rep ^ rep_bit, shard ^ shard_bit),
            device_id_type=pl.DeviceIdType.MESH,
        )

    loads = {}
    for kind, (src, dst) in enumerate(((inner, inner_v), (outer, outer_v), (moment, moment_v))):
        for m in range(len(src)):
            loads[kind, m] = pltpu.make_async_copy(src[m], dst[m], load_sem.at[kind, m])
            loads[kind, m].start()

    barrier = pltpu.get_barrier_semaphore()
    shard_bits = [1 << i for i in range(shards.bit_length() - 1)]
    greet = [(1, 0), (2, 0)] + [(0, bit) for bit in shard_bits]
    for rep_bit, shard_bit in greet:
        pl.semaphore_signal(
            barrier,
            inc=1,
            device_id=(rep ^ rep_bit, shard ^ shard_bit),
            device_id_type=pl.DeviceIdType.MESH,
        )
    pl.semaphore_wait(barrier, len(greet))

    sends, stores = [], []

    def go(copy):
        copy.start()
        sends.append(copy)
        return copy

    def store(src, dst, kind, m):
        copy = pltpu.make_async_copy(src, dst, store_sem.at[kind, m])
        copy.start()
        stores.append(copy)

    first, second = (1, 2), (2, 1)
    step = 16

    def sizes(m):
        rows, width = own[m].shape
        return rows // 2, width

    def columns(owner, width):
        return pl.ds(pl.multiple_of(owner * width, 128), width)

    def over_rows(rows, body):
        def one(i, carry):
            body(pl.multiple_of(i * step, step))
            return carry

        lax.fori_loop(0, rows // step, one, 0)

    def phase_a(m):
        half, width = sizes(m)
        loads[0, m].wait()
        out = []
        for p in range(2):
            def body(at, p=p):
                low = pl.ds(pl.multiple_of(p * half + at, step), step)
                for k, owner in enumerate((rep ^ 3, rep ^ first[p])):
                    to = pl.ds(pl.multiple_of(k * half + at, step), step)
                    send1[m][p, to, :] = pack(inner_v[m][low, columns(owner, width)], inner_limit)

            over_rows(half, body)
            out.append(go(remote(send1[m].at[p], recv1[m].at[p], rs1, (m, p), first[p])))
        return out

    def phase_b(m, came):
        half, width = sizes(m)
        out = []
        for p in range(2):
            came[p].wait_recv()

            def body(at, p=p):
                low = pl.ds(pl.multiple_of(p * half + at, step), step)
                to = pl.ds(at, step)
                relay = inner_v[m][low, columns(rep ^ second[p], width)]
                relay = relay + unpack(recv1[m][p, to, :], inner_limit)
                recv1[m][p, to, :] = pack(relay, 2 * inner_limit)

            over_rows(half, body)
            src = recv1[m].at[p, pl.ds(0, half)]
            out.append(go(remote(src, recv2[m].at[p], rs2, (m, p), second[p])))
        return out

    def spread(m, p):
        half, _ = sizes(m)
        rows = pl.ds(p * half, half)
        x = go(remote(own[m].at[rows], by_x[m].at[rows], agx, (m, p), 1))
        y = go(remote(own[m].at[rows], by_y[m].at[rows], agy, (m, p), 2))
        return x, y

    def update(m, low, delta):
        outer_now = outer_v[m][low, :]
        moment_new = decay_moment * moment_v[m][low, :] + delta
        master_new = outer_now - rate_outer * (delta + decay_moment * moment_new)
        own[m][low, :] = master_new.astype(jnp.bfloat16)
        outer_v[m][low, :] = master_new
        moment_v[m][low, :] = moment_new

    def keep(m):
        _, width = sizes(m)
        store(outer_v[m], master[m], 0, m)
        store(moment_v[m], momentum[m], 1, m)
        store(own[m], weights[m].at[:, columns(rep, width)], 2, m)

    def phase_c(m, came):
        half, width = sizes(m)
        loads[1, m].wait()
        loads[2, m].wait()
        out = []
        for p in range(2):
            came[p].wait_recv()

            def body(at, p=p):
                low = pl.ds(pl.multiple_of(p * half + at, step), step)
                near = pl.ds(pl.multiple_of(half + at, step), step)
                total = inner_v[m][low, columns(rep, width)]
                total = total + unpack(recv1[m][p, near, :], inner_limit)
                total = total + unpack(recv2[m][p, pl.ds(at, step), :], 2 * inner_limit)
                update(m, low, outer_v[m][low, :] - total * (1.0 / groups))

            over_rows(half, body)
            out.append(spread(m, p))
        keep(m)
        return out

    def forward(m, out):
        half, _ = sizes(m)
        top, low = pl.ds(0, half), pl.ds(half, half)
        out[0][0].wait_recv()
        a = go(remote(by_x[m].at[top], far[m].at[top], agf, (m, 0), 2))
        out[1][1].wait_recv()
        b = go(remote(by_y[m].at[low], far[m].at[low], agf, (m, 1), 1))
        return a, b

    def finish(m, out, far_out):
        _, width = sizes(m)
        out[1][0].wait_recv()
        store(by_x[m], weights[m].at[:, columns(rep ^ 1, width)], 3, m)
        out[0][1].wait_recv()
        store(by_y[m], weights[m].at[:, columns(rep ^ 2, width)], 4, m)
        far_out[0].wait_recv()
        far_out[1].wait_recv()
        store(far[m], weights[m].at[:, columns(rep ^ 3, width)], 5, m)

    thin = terms[0].shape[1]

    def coeff_a():
        out = []
        for p in range(2):
            for k, owner in enumerate((rep ^ 3, rep ^ first[p])):
                src = parts[p].at[:, columns(owner, thin)]
                out.append(go(remote(src, c_recv1.at[p, k], c1, (p, k), first[p])))
        return out

    def coeff_b(came):
        out = []
        for p in range(2):
            came[2 * p].wait_recv()
            mine = parts[p][:, columns(rep ^ second[p], thin)]
            c_relay[p] = mine + c_recv1[p, 0]
            out.append(go(remote(c_relay.at[p], c_recv2.at[p], c2, p, second[p])))
        return out

    even = shard % 2 == 0

    def hop(slot, bit):
        return go(remote(s_send.at[slot], s_recv.at[slot], sh, slot, 0, bit))

    def coeff_c(came, later):
        both = []
        for p in range(2):
            came[2 * p + 1].wait_recv()
            later[p].wait_recv()
            total = parts[p][:, columns(rep, thin)] + c_recv1[p, 1] + c_recv2[p]
            both.append(terms[p][...] - total * (1.0 / groups))
        s_send[0] = jnp.where(even, both[1], both[0])
        s_send[1] = jnp.where(even, both[0], both[1])
        return hop(0, 1)

    def coeff_d(slot, came, bit):
        came.wait_recv()
        if slot == 1:
            s_send[1] = s_send[1] + s_recv[0]
        else:
            s_send[slot] = s_send[slot - 1] + s_recv[slot - 1]
        return hop(slot, bit)

    def coeff_f(came):
        came.wait_recv()
        last = len(shard_bits)
        mine, other = s_send[last], s_recv[last]
        coeffs = (jnp.where(even, mine, other), jnp.where(even, other, mine))
        outs = []
        for p, m in ((0, 3), (1, 4)):
            loads[1, m].wait()
            loads[2, m].wait()
            rows = own[m].shape[0]
            block = math.gcd(rows, 128)
            coeff = coeffs[p]

            def one(i, carry, p=p, m=m, coeff=coeff, block=block):
                low = pl.ds(pl.multiple_of(i * block, block), block)
                update(m, low, rebuild(basis[p][low, :], coeff))
                return carry

            lax.fori_loop(0, rows // block, one, 0)
            outs.append([spread(m, 0), spread(m, 1)])
            keep(m)
        return outs

    a0 = phase_a(0)
    ca = coeff_a()
    a1 = phase_a(1)
    cb = coeff_b(ca)
    a2 = phase_a(2)
    hopped = coeff_c(ca, cb)
    b0 = phase_b(0, a0)
    hops = shard_bits[1:] + [1]
    hopped = coeff_d(1, hopped, hops[0])
    b1 = phase_b(1, a1)
    for slot, bit in list(enumerate(hops, 1))[1:-1]:
        hopped = coeff_d(slot, hopped, bit)
    g0 = phase_c(0, b0)
    if len(hops) > 1:
        hopped = coeff_d(len(hops), hopped, hops[-1])
    b2 = phase_b(2, a2)
    g3, g4 = coeff_f(hopped)
    f0 = forward(0, g0)
    g1 = phase_c(1, b1)
    f3 = forward(3, g3)
    f4 = forward(4, g4)
    g2 = phase_c(2, b2)
    f1 = forward(1, g1)
    finish(0, g0, f0)
    finish(3, g3, f3)
    finish(4, g4, f4)
    f2 = forward(2, g2)
    finish(1, g1, f1)
    finish(2, g2, f2)
    for copy in sends:
        copy.wait_send()
    for copy in stores:
        copy.wait()


def fused(inner, outer, moment, parts, terms, basis):
    groups, shards = lax.axis_size("rep"), lax.axis_size("shard")
    f32, bf16 = jnp.float32, jnp.bfloat16
    anywhere = pl.BlockSpec(memory_space=pl.ANY)
    local = pl.BlockSpec(memory_space=pltpu.VMEM)
    own = [x.shape for x in outer]
    code = [(2, x.shape[0], x.shape[1] // groups) for x in inner]
    half = [(2, x.shape[0] // 2, x.shape[1] // groups) for x in inner]
    thin = terms[0].shape
    hops = shards.bit_length()
    vm, dma = pltpu.VMEM, pltpu.SemaphoreType.DMA
    scratch = [vm(x.shape, f32) for x in inner]
    scratch += [vm(x, f32) for x in own + own]
    scratch += [vm(x, bf16) for x in code + code + half + own * 4]
    scratch += [vm((2, 2) + thin, f32), vm((2,) + thin, f32), vm((2,) + thin, f32)]
    scratch += [vm((hops,) + thin, f32), vm((hops,) + thin, f32)]
    scratch += [dma((3, 5)), dma((6, 5))]
    for shape in ((3, 2), (3, 2), (2, 2), (2,), (hops,), (5, 2), (5, 2), (5, 2)):
        scratch += [dma(shape), dma(shape)]
    wide = [jax.ShapeDtypeStruct((x[0], x[1] * groups), bf16) for x in own]
    slim = [jax.ShapeDtypeStruct(x, f32) for x in own]
    return pl.pallas_call(
        functools.partial(fused_kernel, groups, shards),
        out_shape=wide + slim + slim,
        in_specs=[anywhere] * 13 + [local] * 6,
        out_specs=[anywhere] * 15,
        scratch_shapes=scratch,
        compiler_params=pltpu.CompilerParams(
            collective_id=0, has_side_effects=True, vmem_limit_bytes=60 * 2**20
        ),
        cost_estimate=pl.CostEstimate(
            flops=10**9, bytes_accessed=60 * 2**20, transcendentals=10**7
        ),
    )(*inner, *outer, *moment, *parts, *terms, *basis)


def on_device(
    inner_wqkv,
    inner_w1,
    inner_w3,
    inner_wo,
    inner_w2,
    outer_wqkv,
    outer_w1,
    outer_w3,
    outer_wo,
    outer_w2,
    moment_wqkv,
    moment_w1,
    moment_w3,
    moment_wo,
    moment_w2,
    basis_wo,
    basis_w2,
):
    shards = lax.axis_size("shard")
    if lax.axis_size("rep") == 4 and shards > 1 and not shards & (shards - 1):
        return fused(
            (inner_wqkv[0], inner_w1[0], inner_w3[0]),
            (outer_wqkv, outer_w1, outer_w3, outer_wo, outer_w2),
            (moment_wqkv, moment_w1, moment_w3, moment_wo, moment_w2),
            (project(basis_wo, inner_wo[0]), project(basis_w2, inner_w2[0])),
            (project(basis_wo, outer_wo), project(basis_w2, outer_w2)),
            (basis_wo, basis_w2),
        )
    groups = lax.axis_size("rep")
    d_qkv = outer_wqkv - sum_columns(inner_wqkv[0]) / groups
    coeff_out, coeff_down = coefficients(
        inner_wo[0], inner_w2[0], outer_wo, outer_w2, basis_wo, basis_w2
    )
    d_one = outer_w1 - sum_columns(inner_w1[0]) / groups
    d_three = outer_w3 - sum_columns(inner_w3[0]) / groups
    d_out = rebuild(basis_wo, coeff_out)
    d_down = rebuild(basis_w2, coeff_down)
    a0, b0, c0 = nesterov(outer_wqkv, moment_wqkv, d_qkv)
    a1, b1, c1 = nesterov(outer_w1, moment_w1, d_one)
    a3, b3, c3 = nesterov(outer_w3, moment_w3, d_three)
    ao, bo, co = nesterov(outer_wo, moment_wo, d_out)
    a2, b2, c2 = nesterov(outer_w2, moment_w2, d_down)
    (w0,) = gather_columns(a0)
    wo, w2 = gather_columns(ao, a2)
    (w1,) = gather_columns(a1)
    (w3,) = gather_columns(a3)
    return (
        w0,
        w1,
        w3,
        wo,
        w2,
        b0,
        b1,
        b3,
        bo,
        b2,
        c0,
        c1,
        c3,
        co,
        c2,
    )


def solution(mesh):
    inner = P("rep", "shard", None)
    owned = P("shard", "rep")
    shared = P("shard", None)
    return jax.shard_map(
        on_device,
        mesh=mesh,
        in_specs=(inner,) * 5 + (owned,) * 10 + (shared,) * 2,
        out_specs=(shared,) * 5 + (owned,) * 10,
        check_vma=False,
    )
```
